32 devices in a mesh: parts: 2 (over x), tm: 8 (over z, y), panel: 2 (over core).
Axes of the slice: x: 2, y: 2, z: 4, core: 2. Of those that a mesh axis runs over, the one named last changes fastest.
Arguments:
- gain: bfloat16 [16, 1024, 1024], P(('parts', 'tm'), 'panel'), parts along dimension 0, may hold values from -0.1875 to 0.1875
- offset: bfloat16 [16, 1024], P(('parts', 'tm')), parts along dimension 0, may hold values from -3 to 3
- residual_cov: bfloat16 [16, 1024, 1024], P(('parts', 'tm'), 'panel'), parts along dimension 0, may hold values from -9 to 9, as said below
Outputs:
- smoothed_mean: bfloat16 [16, 1024], P(('parts', 'tm')), parts along dimension 0
- smoothed_cov: bfloat16 [16, 1024, 1024], P(('parts', 'tm'), 'panel'), parts along dimension 0
The draws below stay inside these ranges and needn't reach their ends.
There are 2 independent parts, one for each index of `parts`. The reference program is written for one: setup_inputs(seed, part) draws one part's arguments, and reference() takes and returns one part's arrays. A program takes and returns all parts, laid end to end along the dimension named above; each array names one. Nothing has to cross between parts.
Inputs may be any that keep to these rules, and one draw needn't show every extreme that they name: Each block residual_cov[k] is a symmetric matrix.
All inputs are finite; a program needn't handle non-finite values.
Results may differ from the reference program's by a relative error of at most 0.0062.
Values may be sent and summed in bfloat16 or wider, within the bound.
A program may use at most 128 MiB of HBM per device.

```python
import math
import jax
import jax.numpy as jnp
from jax import lax

STATE = 1024
STEPS = 8


def draw_residual_cov(key, part):
    base = jax.random.fold_in(key, 11)
    first, second = jax.random.split(base, 2)
    diag = jax.random.uniform(first, (STEPS, STATE), jnp.float32, 1.0, 2.0)
    noise = jax.random.normal(second, (STEPS, STATE, STATE), jnp.float32)
    sym = (noise + jnp.swapaxes(noise, 1, 2)) * (0.35 / math.sqrt(2.0 * STATE))
    ident = jnp.eye(STATE, dtype=jnp.float32)
    block = 0.25 * (sym + ident[None] * diag[:, :, None])
    return block.astype(jnp.bfloat16)


def steps_of(own_key, extent, shards, least, high):
    def one(axis_at, shards_of):
        heights = jax.random.uniform(jax.random.fold_in(jax.random.fold_in(own_key, 6), axis_at), (shards_of,), jnp.float32, least / len(shards), high / len(shards))
        return jnp.repeat(jnp.exp(heights), extent[axis_at] // shards_of).reshape((-1,) + (1,) * (len(extent) - axis_at - 1))

    level = one(*shards[0])
    for cut in shards[1:]:
        level = level * one(*cut)
    return level


def normal_values(key, extent, deviation, bound, cuts=(), held_as=jnp.bfloat16):
    entries = jax.random.normal(key, extent, jnp.float32) * deviation
    if len(cuts) > 0:
        entries = steps_of(key, extent, cuts, -0.22, 0.18) * entries
    return jnp.clip(entries, min=-bound, max=bound).astype(held_as)


def setup_inputs(seed: int = 0, part: int = 0) -> dict:
    streams_of = jax.random.split(jax.random.key(seed), 4)
    part_splits = jax.random.split(jax.random.fold_in(streams_of[3], part), 4)
    gain = normal_values(part_splits[0], (STEPS, STATE, STATE), (STATE * 17 // 16) ** -0.5, 0.1875, ((0, 8), (1, 2)))
    offset = normal_values(part_splits[1], (STEPS, STATE), 0.5, 3.0, ((0, 8),))
    residual_cov = draw_residual_cov(jax.random.fold_in(jax.random.fold_in(streams_of[3], part), 71), part)
    return dict(gain=gain, offset=offset, residual_cov=residual_cov)


def reference(gain, offset, residual_cov):
    steps = gain.shape[0]
    width = gain.shape[1]
    keep = (jnp.arange(steps) < steps - 1).astype(jnp.float32)
    gains = (gain.astype(jnp.float32) * keep[:, None, None]).astype(jnp.bfloat16)
    offs = offset
    covs = residual_cov
    levels = (steps - 1).bit_length()
    high = lax.Precision.HIGHEST
    for level in range(levels):
        dist = 1 << level
        pad_block = jnp.zeros((dist, width, width), jnp.bfloat16)
        pad_row = jnp.zeros((dist, width), jnp.bfloat16)
        far_gain = jnp.concatenate([gains[dist:], pad_block], axis=0)
        far_cov = jnp.concatenate([covs[dist:], pad_block], axis=0)
        far_off = jnp.concatenate([offs[dist:], pad_row], axis=0)
        own = gains.astype(jnp.float32)
        cross = jnp.einsum("kij,kjl->kil", own, far_cov.astype(jnp.float32), precision=high).astype(jnp.bfloat16)
        new_cov = jnp.einsum("kij,klj->kil", cross.astype(jnp.float32), own, precision=high) + covs.astype(jnp.float32)
        new_off = jnp.einsum("kij,kj->ki", own, far_off.astype(jnp.float32), precision=high) + offs.astype(jnp.float32)
        if level < levels - 1:
            gains = jnp.einsum("kij,kjl->kil", own, far_gain.astype(jnp.float32), precision=high).astype(jnp.bfloat16)
        covs = new_cov.astype(jnp.bfloat16)
        offs = new_off.astype(jnp.bfloat16)
    return offs, covs
```

```python
import functools

import jax
import jax.numpy as jnp
from jax import lax
from jax.experimental import pallas as pl
from jax.experimental.pallas import tpu as pltpu
from jax.sharding import PartitionSpec as P

OWNED = (((0, 0), (0, 1), (1, 1), (1, 2), (0, 2)), ((0, 0), (0, 1), (1, 1), (1, 2), (1, 3)))
CHUNKS = 4


def block_table():
    table = {}
    for core in range(2):
        for slot, (row, col) in enumerate(OWNED[core]):
            table[(2 * core + row, (2 * core + col) % 4)] = (core, slot)
    return table


TABLE = block_table()


def dot(a, b):
    return jnp.dot(a, b, preferred_element_type=jnp.float32)


def dot_t(a, b):
    return lax.dot_general(a, b, (((1,), (1,)), ((), ())), preferred_element_type=jnp.float32)


def to_tile(row):
    lanes = row.shape[1] // 8
    return jnp.concatenate([row[:, i * lanes : (i + 1) * lanes] for i in range(8)], axis=0)


def to_row(tile):
    return jnp.concatenate([tile[i : i + 1, :] for i in range(8)], axis=1)


def kernel(
    steps, gain, offset, cov, mean_out, cov_out,
    own, far, weight, near_cov, chain_cov, near_g, chain_g, sent_g, cross, added, added_g,
    s_own, r_own, s_far, r_far, s_farx, r_farx, s_near, r_near, s_nearx, r_nearx,
    s_prod, r_prod, s_chain, r_chain, s_chainx, r_chainx, s_side,
):
    t = lax.axis_index("tm")
    c = lax.axis_index("panel")
    z = t // 2
    y = t % 2
    last_z = steps // 2 - 1
    width = gain.shape[1]
    half = width // 2
    bs = width // 4
    cr = half // CHUNKS

    core = {"panel": 1 - c}
    side = {"tm": t + 1 - 2 * y}
    above = {"tm": t + 2}
    below = {"tm": t - 2}

    barrier = pltpu.get_barrier_semaphore()
    even = y == 0
    top = z == last_z
    pl.semaphore_signal(barrier, inc=1, device_id=core)
    pl.semaphore_signal(barrier, inc=1, device_id=side)

    @pl.when(jnp.logical_and(even, z < last_z))
    def _():
        pl.semaphore_signal(barrier, inc=1, device_id=above)

    @pl.when(jnp.logical_and(even, z > 0))
    def _():
        pl.semaphore_signal(barrier, inc=1, device_id=below)

    has_above = jnp.where(jnp.logical_and(even, z < last_z), 1, 0)
    has_below = jnp.where(jnp.logical_and(even, z > 0), 1, 0)
    pl.semaphore_wait(barrier, 2 + has_above + has_below)

    def remote(src, dst, send, recv, device):
        return pltpu.make_async_remote_copy(
            src_ref=src, dst_ref=dst, send_sem=send, recv_sem=recv,
            device_id=device, device_id_type=pl.DeviceIdType.MESH,
        )

    def cut(ref, slot):
        if OWNED[0][slot] == OWNED[1][slot]:
            row, col = OWNED[0][slot]
        else:
            (r0, c0), (r1, c1) = OWNED[0][slot], OWNED[1][slot]
            row, col = r0 + (r1 - r0) * c, c0 + (c1 - c0) * c
        start = pl.multiple_of(((col + 2 * c) % 4) * bs, bs)
        return ref.at[pl.ds(pl.multiple_of(row * bs, bs), bs), pl.ds(start, bs)]

    def far_copy(i):
        rows = pl.ds(i * cr, cr)
        return remote(gain.at[rows], far.at[c, rows], s_far.at[i], r_far.at[i], side)

    def far_cross(i, slot):
        rows = pl.ds(i * cr, cr)
        return remote(far.at[slot, rows], far.at[slot, rows], s_farx.at[i], r_farx.at[i], core)

    def near_copy(b):
        return remote(cut(cov, b), near_cov.at[c, b], s_near.at[b], r_near.at[b], side)

    def near_g_copy():
        return remote(sent_g, near_g, s_near.at[5], r_near.at[5], side)

    def near_cross(b, slot):
        return remote(near_cov.at[slot, b], near_cov.at[slot, b], s_nearx.at[b], r_nearx.at[b], core)

    def prod_cross(n, slot):
        cols = pl.ds(n * bs, bs)
        return remote(weight.at[slot, :, cols], weight.at[slot, :, cols], s_prod.at[n], r_prod.at[n], core)

    def chain_copy(b):
        return remote(cut(cov_out, b), chain_cov.at[c, b], s_chain.at[b], r_chain.at[b], below)

    def chain_g_copy():
        return remote(sent_g, chain_g, s_chain.at[5], r_chain.at[5], below)

    def chain_side(b):
        return remote(chain_cov.at[c, b], chain_cov.at[c, b], s_side.at[b], r_chain.at[b], side)

    def chain_g_side():
        return remote(chain_g, chain_g, s_side.at[5], r_chain.at[5], side)

    def chain_cross(b, slot):
        return remote(chain_cov.at[slot, b], chain_cov.at[slot, b], s_chainx.at[b], r_chainx.at[b], core)

    def combine(left, left_rows, later, later_g, emit, emit_g):
        for j in range(4):
            total = None
            for i in range(4):
                piece = left_rows[:, i * bs : (i + 1) * bs]
                if (i, j) in TABLE:
                    term = dot(piece, later[TABLE[(i, j)]])
                else:
                    term = dot_t(piece, later[TABLE[(j, i)]])
                total = term if total is None else total + term
            cross[:half, j * bs : (j + 1) * bs] = total.astype(jnp.bfloat16)
        row = to_row(later_g[...]).astype(jnp.bfloat16)
        cross[half:, :] = jnp.broadcast_to(row, (16, width))
        for n in range(4):
            panel = (n // 2 + c) % 2
            cols = pl.ds(pl.multiple_of(((n + 2 * c) % 4) * bs, bs), bs)
            rows = left[panel, (n % 2) * bs : (n % 2 + 1) * bs, :]
            out = dot_t(cross[...], rows)
            emit(n, cols, out[:half])
            emit_g(cols, out[half : half + 1])

    def finish(left, left_rows, later, later_g, add, add_g):
        go_down = jnp.logical_and(even, z > 0)

        def emit(n, cols, value):
            cov_out[:, cols] = (value + add(cols)).astype(jnp.bfloat16)
            ready = ((0,), (1, 2), (3,), (4,))[n]

            @pl.when(go_down)
            def _():
                for b in ready:
                    chain_copy(b).start()

        def emit_g(cols, value):
            added_g[:, cols] = value + add_g(cols)

        combine(left, left_rows, later, later_g, emit, emit_g)
        mean_out[...] = added_g[...].astype(jnp.bfloat16)

        @pl.when(go_down)
        def _():
            sent_g[...] = to_tile(added_g[...])
            chain_g_copy().start()
            for b in range(5):
                chain_copy(b).wait_send()
            chain_g_copy().wait_send()

    @pl.when(y == 1)
    def _():
        sent_g[...] = to_tile(offset[...].astype(jnp.float32))

        @pl.when(z < last_z)
        def _():
            for i in range(CHUNKS):
                far_copy(i).start()

        for b in range(5):
            near_copy(b).start()
        near_g_copy().start()

        @pl.when(top)
        def _():
            cov_out[...] = cov[...]
            mean_out[...] = offset[...]

        @pl.when(z < last_z)
        def _():
            swap = remote(gain, weight.at[c], s_own.at[0], r_own.at[0], core)
            swap.start()
            weight[c] = gain[...]
            added[...] = cov[...].astype(jnp.float32)
            added_g[...] = offset[...].astype(jnp.float32)
            swap.wait()

    @pl.when(even)
    def _():
        swap = remote(gain, own.at[c], s_own.at[0], r_own.at[0], core)
        swap.start()
        own[c] = gain[...]

        @pl.when(z < last_z)
        def _():
            for i in range(CHUNKS):
                far_copy(i).wait_recv()
                far_cross(i, c).start()
            for i in range(CHUNKS):
                far_cross(i, 1 - c).wait_recv()
            for n in range(4):
                cols = slice(n * bs, (n + 1) * bs)
                value = dot(gain[:, :half], far[0, :, cols]) + dot(gain[:, half:], far[1, :, cols])
                weight[c, :, cols] = value.astype(jnp.bfloat16)
                prod_cross(n, c).start()

        swap.wait()
        for b in range(5):
            near_copy(b).wait_recv()
            near_cross(b, c).start()
        near_g_copy().wait_recv()
        for b in range(5):
            near_cross(b, 1 - c).wait_recv()

        @pl.when(z < last_z)
        def _():
            def emit(n, cols, value):
                added[:, cols] = value + cov[:, cols].astype(jnp.float32)

            def emit_g(cols, value):
                added_g[:, cols] = value + offset[:, cols].astype(jnp.float32)

            combine(own, gain[...], near_cov, near_g, emit, emit_g)

        @pl.when(top)
        def _():
            finish(
                own, gain[...], near_cov, near_g,
                lambda cols: cov[:, cols].astype(jnp.float32),
                lambda cols: offset[:, cols].astype(jnp.float32),
            )

    @pl.when(z < last_z)
    def _():
        for b in range(5):
            chain_copy(b).wait_recv()
            chain_cross(b, c).start()

            @pl.when(even)
            def _():
                chain_side(b).start()

        chain_g_copy().wait_recv()

        @pl.when(even)
        def _():
            chain_g_side().start()
            for n in range(4):
                prod_cross(n, 1 - c).wait_recv()

        for b in range(5):
            chain_cross(b, 1 - c).wait_recv()
        finish(
            weight, weight[c], chain_cov, chain_g,
            lambda cols: added[:, cols], lambda cols: added_g[:, cols],
        )
        for b in range(5):
            chain_cross(b, c).wait_send()

        @pl.when(even)
        def _():
            for b in range(5):
                chain_side(b).wait_send()
            chain_g_side().wait_send()
            for n in range(4):
                prod_cross(n, c).wait_send()
            for i in range(CHUNKS):
                far_cross(i, c).wait_send()

        @pl.when(y == 1)
        def _():
            for i in range(CHUNKS):
                far_copy(i).wait_send()

    @pl.when(y == 1)
    def _():
        for b in range(5):
            near_copy(b).wait_send()
        near_g_copy().wait_send()

    @pl.when(even)
    def _():
        for b in range(5):
            near_cross(b, c).wait_send()


def body(gain, offset, residual_cov):
    steps = lax.axis_size("tm")
    _, half, width = gain.shape
    bs = width // 4
    bf16, f32 = jnp.bfloat16, jnp.float32
    vmem = pl.BlockSpec(memory_space=pltpu.VMEM)
    counts = (1, 1, CHUNKS, CHUNKS, CHUNKS, CHUNKS, 6, 6, 5, 5, 4, 4, 6, 6, 5, 5, 6)
    mean, cov = pl.pallas_call(
        functools.partial(kernel, steps),
        out_shape=(
            jax.ShapeDtypeStruct((1, width), bf16),
            jax.ShapeDtypeStruct((half, width), bf16),
        ),
        in_specs=[vmem] * 3,
        out_specs=(vmem, vmem),
        scratch_shapes=[
            pltpu.VMEM((2, half, width), bf16),
            pltpu.VMEM((2, half, width), bf16),
            pltpu.VMEM((2, half, width), bf16),
            pltpu.VMEM((2, 5, bs, bs), bf16),
            pltpu.VMEM((2, 5, bs, bs), bf16),
            pltpu.VMEM((8, width // 8), f32),
            pltpu.VMEM((8, width // 8), f32),
            pltpu.VMEM((8, width // 8), f32),
            pltpu.VMEM((half + 16, width), bf16),
            pltpu.VMEM((half, width), f32),
            pltpu.VMEM((1, width), f32),
        ]
        + [pltpu.SemaphoreType.DMA((n,)) for n in counts],
        compiler_params=pltpu.CompilerParams(
            collective_id=0, has_side_effects=True, vmem_limit_bytes=40 * 2**20
        ),
        cost_estimate=pl.CostEstimate(
            flops=10 * half * width * width, bytes_accessed=6 * half * width, transcendentals=0
        ),
    )(gain[0], offset, residual_cov[0])
    return mean, cov[None]


def solution(mesh):
    in_specs = (
        P(("parts", "tm"), "panel", None),
        P(("parts", "tm"), None),
        P(("parts", "tm"), "panel", None),
    )
    out_specs = (P(("parts", "tm"), None), P(("parts", "tm"), "panel", None))
    return jax.shard_map(body, mesh=mesh, in_specs=in_specs, out_specs=out_specs, check_vma=False)
```

```python
import functools

import jax
import jax.numpy as jnp
from jax import lax
from jax.experimental import pallas as pl
from jax.experimental.pallas import tpu as pltpu
from jax.sharding import PartitionSpec as P

OWNED = (((0, 0), (0, 1), (1, 1), (1, 2), (0, 2)), ((0, 0), (0, 1), (1, 1), (1, 2), (1, 3)))
CHUNKS = 4
UNITS = 10
DIAGONAL = (0, 2)
ROUND = (0, 1, 2, 3)
DIRECT = (4, 5, 6, 7, 8, 9)
EVEN_ORDER = (4, 5, 6, 0, 7, 1, 8, 2, 9, 3)
ODD_ORDER = (0, 1, 4, 2, 5, 3, 6, 7, 8, 9)


def block_table():
    table = {}
    for core in range(2):
        for slot, (row, col) in enumerate(OWNED[core]):
            table[(2 * core + row, (2 * core + col) % 4)] = (core, slot)
    return table


TABLE = block_table()


def dot(a, b):
    return jnp.dot(a, b, preferred_element_type=jnp.float32)


def dot_t(a, b):
    return lax.dot_general(a, b, (((1,), (1,)), ((), ())), preferred_element_type=jnp.float32)


def to_tile(row):
    lanes = row.shape[1] // 8
    return jnp.concatenate([row[:, i * lanes : (i + 1) * lanes] for i in range(8)], axis=0)


def to_row(tile):
    return jnp.concatenate([tile[i : i + 1, :] for i in range(8)], axis=1)


def kernel(
    steps, gain_in, offset, cov_in, mean_out, cov_out,
    own, far, weight, near_cov, chain_cov, relay_cov, cov,
    near_g, chain_g, sent_g, cross, added, added_g,
    s_local, s_own, r_own, s_far, r_far, s_farx, r_farx, s_near, r_near, s_nearx, r_nearx,
    s_prod, r_prod, s_chain, r_chain, s_chainx, r_chainx, s_side, s_relay, r_relay,
):
    t = lax.axis_index("tm")
    c = lax.axis_index("panel")
    z = t // 2
    y = t % 2
    last_z = steps // 2 - 1
    half, width = cov.shape
    bs = width // 4
    hb = bs // 2
    cr = half // CHUNKS

    core = {"panel": 1 - c}
    side = {"tm": t + 1 - 2 * y}
    above = {"tm": t + 2}
    below = {"tm": t - 2}
    even = y == 0
    odd = y == 1
    top = z == last_z
    second = z == last_z - 1

    load_cov = pltpu.make_async_copy(cov_in, cov, s_local.at[0])
    load_cov.start()

    @pl.when(even)
    def _():
        pltpu.make_async_copy(gain_in, own.at[c], s_local.at[1]).start()

    @pl.when(odd)
    def _():
        pltpu.make_async_copy(gain_in, weight.at[c], s_local.at[1]).start()

    barrier = pltpu.get_barrier_semaphore()
    pl.semaphore_signal(barrier, inc=1, device_id=core)
    pl.semaphore_signal(barrier, inc=1, device_id=side)

    @pl.when(z < last_z)
    def _():
        pl.semaphore_signal(barrier, inc=1, device_id=above)

    @pl.when(z > 0)
    def _():
        pl.semaphore_signal(barrier, inc=1, device_id=below)

    pl.semaphore_wait(barrier, 2 + jnp.where(z < last_z, 1, 0) + jnp.where(z > 0, 1, 0))

    def remote(src, dst, send, recv, device):
        return pltpu.make_async_remote_copy(
            src_ref=src, dst_ref=dst, send_sem=send, recv_sem=recv,
            device_id=device, device_id_type=pl.DeviceIdType.MESH,
        )

    def skipped(u):
        return hb if u // 2 in DIAGONAL and u % 2 == 1 else 0

    def cut(ref, u):
        slot, low = u // 2, u % 2
        (r0, c0), (r1, c1) = OWNED[0][slot], OWNED[1][slot]
        row = r0 if r0 == r1 else r0 + (r1 - r0) * c
        col = c0 if c0 == c1 else c0 + (c1 - c0) * c
        skip = skipped(u)
        start = pl.multiple_of(((col + 2 * c) % 4) * bs + skip, hb)
        return ref.at[pl.ds(pl.multiple_of(row * bs + low * hb, hb), hb), pl.ds(start, bs - skip)]

    def unit(ref, owner, u):
        skip = skipped(u)
        return ref.at[owner, u // 2, pl.ds(u % 2 * hb, hb), pl.ds(skip, bs - skip)]

    def relay_unit(u):
        skip = skipped(u)
        return relay_cov.at[u // 2, pl.ds(u % 2 * hb, hb), pl.ds(skip, bs - skip)]

    def far_copy(i):
        rows = pl.ds(i * cr, cr)
        return remote(gain_in.at[rows], far.at[c, rows], s_far.at[i], r_far.at[i], side)

    def far_cross(i, slot):
        rows = pl.ds(i * cr, cr)
        return remote(far.at[slot, rows], far.at[slot, rows], s_farx.at[i], r_farx.at[i], core)

    def near_copy(u):
        return remote(cut(cov_in, u), unit(near_cov, c, u), s_near.at[u], r_near.at[u], side)

    def near_g_copy():
        return remote(sent_g, near_g, s_near.at[UNITS], r_near.at[UNITS], side)

    def near_cross(u, owner):
        part = unit(near_cov, owner, u)
        return remote(part, part, s_nearx.at[u], r_nearx.at[u], core)

    def prod_cross(n, slot):
        cols = pl.ds(n * bs, bs)
        return remote(weight.at[slot, :, cols], weight.at[slot, :, cols], s_prod.at[n], r_prod.at[n], core)

    def chain_copy(u):
        return remote(cut(cov_out, u), unit(chain_cov, c, u), s_chain.at[u], r_chain.at[u], below)

    def relay_copy(u):
        return remote(cut(cov_out, u), relay_unit(u), s_chain.at[u], r_relay.at[u], side)

    def relay_down(u):
        return remote(relay_unit(u), unit(chain_cov, c, u), s_relay.at[u], r_chain.at[u], below)

    def chain_g_copy():
        return remote(sent_g, chain_g, s_chain.at[UNITS], r_chain.at[UNITS], below)

    def chain_side(u):
        part = unit(chain_cov, c, u)
        return remote(part, part, s_side.at[u], r_chain.at[u], side)

    def chain_g_side():
        return remote(chain_g, chain_g, s_side.at[UNITS], r_chain.at[UNITS], side)

    def chain_cross(u, owner):
        part = unit(chain_cov, owner, u)
        return remote(part, part, s_chainx.at[u], r_chainx.at[u], core)

    def combine(left, later, later_g, emit, emit_g):
        for owner in range(2):
            for slot in DIAGONAL:
                later[owner, slot, hb:, :hb] = later[owner, slot, :hb, hb:].T
        for j in range(4):
            total = None
            for i in range(4):
                piece = left[c, :, i * bs : (i + 1) * bs]
                if (i, j) in TABLE:
                    term = dot(piece, later[TABLE[(i, j)]])
                else:
                    term = dot_t(piece, later[TABLE[(j, i)]])
                total = term if total is None else total + term
            cross[:half, j * bs : (j + 1) * bs] = total.astype(jnp.bfloat16)
        row = to_row(later_g[...]).astype(jnp.bfloat16)
        cross[half:, :] = jnp.broadcast_to(row, (16, width))
        for n in range(4):
            panel = (n // 2 + c) % 2
            cols = pl.ds(pl.multiple_of(((n + 2 * c) % 4) * bs, bs), bs)
            rows = left[panel, (n % 2) * bs : (n % 2 + 1) * bs, :]
            out = dot_t(cross[...], rows)
            emit(n, cols, out[:half])
            emit_g(cols, out[half : half + 1])

    def first(left, later, later_g):
        def emit(n, cols, value):
            added[:, cols] = value + cov[:, cols].astype(jnp.float32)

        def emit_g(cols, value):
            added_g[:, cols] = value + offset[:, cols].astype(jnp.float32)

        combine(left, later, later_g, emit, emit_g)

    def finish(left, later, later_g):
        go_down = jnp.logical_and(even, z > 0)
        around = jnp.logical_and(go_down, z < last_z)
        straight = jnp.logical_and(go_down, top)

        def emit(n, cols, value):
            cov_out[:, cols] = (value + added[:, cols]).astype(jnp.bfloat16)
            ready = [2 * slot + low for slot in ((0,), (1, 2), (3,), (4,))[n] for low in range(2)]

            @pl.when(around)
            def _():
                for u in ready:
                    (relay_copy(u) if u in ROUND else chain_copy(u)).start()

            @pl.when(straight)
            def _():
                for u in ready:
                    chain_copy(u).start()

        def emit_g(cols, value):
            added_g[:, cols] = value + added_g[:, cols]

        combine(left, later, later_g, emit, emit_g)
        mean_out[...] = added_g[...].astype(jnp.bfloat16)

        @pl.when(go_down)
        def _():
            sent_g[...] = to_tile(added_g[...])
            chain_g_copy().start()
            for u in range(UNITS):
                chain_copy(u).wait_send()
            chain_g_copy().wait_send()

    def plain_added():
        added[...] = cov[...].astype(jnp.float32)
        added_g[...] = offset[...].astype(jnp.float32)

    def receive(order, forwarded):
        for u in order:
            chain_copy(u).wait_recv()
            chain_cross(u, c).start()
            if u in forwarded:
                chain_side(u).start()

    def receive_near(units):
        for u in units:
            near_copy(u).wait_recv()
            near_cross(u, c).start()

    @pl.when(odd)
    def _():
        sent_g[...] = to_tile(offset[...].astype(jnp.float32))

        @pl.when(z < last_z)
        def _():
            for i in range(CHUNKS):
                far_copy(i).start()

        for u in range(UNITS):
            near_copy(u).start()
        near_g_copy().start()
        load_cov.wait()
        pltpu.make_async_copy(gain_in, weight.at[c], s_local.at[1]).wait()

        @pl.when(top)
        def _():
            cov_out[...] = cov[...]
            mean_out[...] = offset[...]

        @pl.when(z < last_z)
        def _():
            swap = remote(gain_in, weight.at[c], s_own.at[0], r_own.at[0], core)
            swap.start()
            plain_added()
            swap.wait()

            @pl.when(second)
            def _():
                receive(range(UNITS), ())

            @pl.when(jnp.logical_not(second))
            def _():
                receive(ODD_ORDER, ROUND)

            chain_g_copy().wait_recv()

            @pl.when(z > 0)
            def _():
                for u in ROUND:
                    relay_copy(u).wait_recv()
                    relay_down(u).start()

    @pl.when(even)
    def _():
        swap = remote(gain_in, own.at[c], s_own.at[0], r_own.at[0], core)
        swap.start()
        load_cov.wait()
        pltpu.make_async_copy(gain_in, own.at[c], s_local.at[1]).wait()

        @pl.when(z < last_z)
        def _():
            for i in range(CHUNKS):
                far_copy(i).wait_recv()
                far_cross(i, c).start()
            for i in range(CHUNKS):
                far_cross(i, 1 - c).wait_recv()
            for n in range(4):
                cols = slice(n * bs, (n + 1) * bs)
                value = dot(own[c, :, :half], far[0, :, cols]) + dot(own[c, :, half:], far[1, :, cols])
                weight[c, :, cols] = value.astype(jnp.bfloat16)
                prod_cross(n, c).start()

        swap.wait()

        @pl.when(second)
        def _():
            receive(range(UNITS), range(UNITS))
            chain_g_copy().wait_recv()
            chain_g_side().start()
            receive_near(range(5))
            for n in range(4):
                prod_cross(n, 1 - c).wait_recv()
            for u in range(UNITS):
                chain_cross(u, 1 - c).wait_recv()
            first(weight, chain_cov, chain_g)
            receive_near(range(5, UNITS))

        @pl.when(jnp.logical_not(second))
        def _():
            receive_near(range(UNITS))

        near_g_copy().wait_recv()
        for u in range(UNITS):
            near_cross(u, 1 - c).wait_recv()

        @pl.when(z < last_z - 1)
        def _():
            first(own, near_cov, near_g)
            receive(EVEN_ORDER, DIRECT)
            chain_g_copy().wait_recv()
            chain_g_side().start()
            for n in range(4):
                prod_cross(n, 1 - c).wait_recv()

        @pl.when(top)
        def _():
            plain_added()

        @pl.when(z >= last_z - 1)
        def _():
            finish(own, near_cov, near_g)

    @pl.when(jnp.logical_or(z < last_z - 1, jnp.logical_and(odd, second)))
    def _():
        for u in range(UNITS):
            chain_cross(u, 1 - c).wait_recv()
        finish(weight, chain_cov, chain_g)

    @pl.when(z < last_z)
    def _():
        for u in range(UNITS):
            chain_cross(u, c).wait_send()

    @pl.when(even)
    def _():
        for u in range(UNITS):
            near_cross(u, c).wait_send()

        @pl.when(z < last_z)
        def _():
            chain_g_side().wait_send()
            for u in DIRECT:
                chain_side(u).wait_send()
            for n in range(4):
                prod_cross(n, c).wait_send()
            for i in range(CHUNKS):
                far_cross(i, c).wait_send()

        @pl.when(second)
        def _():
            for u in ROUND:
                chain_side(u).wait_send()

    @pl.when(odd)
    def _():
        for u in range(UNITS):
            near_copy(u).wait_send()
        near_g_copy().wait_send()

        @pl.when(z < last_z)
        def _():
            for i in range(CHUNKS):
                far_copy(i).wait_send()

            @pl.when(z > 0)
            def _():
                for u in ROUND:
                    relay_down(u).wait_send()

        @pl.when(z < last_z - 1)
        def _():
            for u in ROUND:
                chain_side(u).wait_send()


def body(gain, offset, residual_cov):
    steps = lax.axis_size("tm")
    _, half, width = gain.shape
    bs = width // 4
    bf16, f32 = jnp.bfloat16, jnp.float32
    hbm = pl.BlockSpec(memory_space=pl.ANY)
    vmem = pl.BlockSpec(memory_space=pltpu.VMEM)
    counts = (2, 1, 1) + (CHUNKS,) * 4 + (UNITS + 1,) * 4 + (4, 4) + (UNITS + 1,) * 7
    mean, cov = pl.pallas_call(
        functools.partial(kernel, steps),
        out_shape=(
            jax.ShapeDtypeStruct((1, width), bf16),
            jax.ShapeDtypeStruct((half, width), bf16),
        ),
        in_specs=[hbm, vmem, hbm],
        out_specs=(vmem, vmem),
        scratch_shapes=[
            pltpu.VMEM((2, half, width), bf16),
            pltpu.VMEM((2, half, width), bf16),
            pltpu.VMEM((2, half, width), bf16),
            pltpu.VMEM((2, 5, bs, bs), bf16),
            pltpu.VMEM((2, 5, bs, bs), bf16),
            pltpu.VMEM((2, bs, bs), bf16),
            pltpu.VMEM((half, width), bf16),
            pltpu.VMEM((8, width // 8), f32),
            pltpu.VMEM((8, width // 8), f32),
            pltpu.VMEM((8, width // 8), f32),
            pltpu.VMEM((half + 16, width), bf16),
            pltpu.VMEM((half, width), f32),
            pltpu.VMEM((1, width), f32),
        ]
        + [pltpu.SemaphoreType.DMA((n,)) for n in counts],
        compiler_params=pltpu.CompilerParams(
            collective_id=0, has_side_effects=True, vmem_limit_bytes=40 * 2**20
        ),
        cost_estimate=pl.CostEstimate(
            flops=10 * half * width * width, bytes_accessed=6 * half * width, transcendentals=0
        ),
    )(gain[0], offset, residual_cov[0])
    return mean, cov[None]


def solution(mesh):
    in_specs = (
        P(("parts", "tm"), "panel", None),
        P(("parts", "tm"), None),
        P(("parts", "tm"), "panel", None),
    )
    out_specs = (P(("parts", "tm"), None), P(("parts", "tm"), "panel", None))
    return jax.shard_map(body, mesh=mesh, in_specs=in_specs, out_specs=out_specs, check_vma=False)
```

```python
import functools

import jax
import jax.numpy as jnp
from jax import lax
from jax.experimental import pallas as pl
from jax.experimental.pallas import tpu as pltpu
from jax.sharding import PartitionSpec as P

OWNED = (((0, 0), (0, 1), (1, 1), (1, 2), (0, 2)), ((0, 0), (0, 1), (1, 1), (1, 2), (1, 3)))
CHUNKS = 4
UNITS = 10
DIAGONAL = (0, 2)
ROUND = (0, 2)
DIRECT = (1, 3, 4, 5, 6, 7, 8, 9)
EVEN_ORDER = (1, 3, 4, 5, 6, 7, 0, 8, 2, 9)
ODD_ORDER = (0, 1, 2, 3, 4, 5, 6, 7, 8, 9)
WINDOW = 3


def block_table():
    table = {}
    for core in range(2):
        for slot, (row, col) in enumerate(OWNED[core]):
            table[(2 * core + row, (2 * core + col) % 4)] = (core, slot)
    return table


TABLE = block_table()


def dot(a, b):
    return jnp.dot(a, b, preferred_element_type=jnp.float32)


def dot_t(a, b):
    return lax.dot_general(a, b, (((1,), (1,)), ((), ())), preferred_element_type=jnp.float32)


def to_tile(row):
    lanes = row.shape[1] // 8
    return jnp.concatenate([row[:, i * lanes : (i + 1) * lanes] for i in range(8)], axis=0)


def to_row(tile):
    return jnp.concatenate([tile[i : i + 1, :] for i in range(8)], axis=1)


def kernel(
    steps, gain_in, offset, cov_in, mean_out, cov_out,
    own, far, weight, near_cov, chain_cov, relay_cov, cov,
    near_g, chain_g, sent_g, cross, added, added_g,
    s_local, s_own, r_own, s_far, r_far, s_farx, r_farx, s_near, r_near, s_nearx, r_nearx,
    s_prod, r_prod, s_chain, r_chain, s_chainx, r_chainx, s_side, s_relay, r_relay,
):
    t = lax.axis_index("tm")
    c = lax.axis_index("panel")
    z = t // 2
    y = t % 2
    last_z = steps // 2 - 1
    half, width = cov.shape
    bs = width // 4
    hb = bs // 2
    cr = half // CHUNKS

    core = {"panel": 1 - c}
    side = {"tm": t + 1 - 2 * y}
    above = {"tm": t + 2}
    below = {"tm": t - 2}
    even = y == 0
    odd = y == 1
    top = z == last_z
    second = z == last_z - 1

    load_cov = pltpu.make_async_copy(cov_in, cov, s_local.at[0])
    load_cov.start()

    @pl.when(even)
    def _():
        pltpu.make_async_copy(gain_in, own.at[c], s_local.at[1]).start()

    @pl.when(odd)
    def _():
        pltpu.make_async_copy(gain_in, weight.at[c], s_local.at[1]).start()

    barrier = pltpu.get_barrier_semaphore()
    pl.semaphore_signal(barrier, inc=1, device_id=core)
    pl.semaphore_signal(barrier, inc=1, device_id=side)

    @pl.when(z < last_z)
    def _():
        pl.semaphore_signal(barrier, inc=1, device_id=above)

    @pl.when(z > 0)
    def _():
        pl.semaphore_signal(barrier, inc=1, device_id=below)

    pl.semaphore_wait(barrier, 2 + jnp.where(z < last_z, 1, 0) + jnp.where(z > 0, 1, 0))

    def remote(src, dst, send, recv, device):
        return pltpu.make_async_remote_copy(
            src_ref=src, dst_ref=dst, send_sem=send, recv_sem=recv,
            device_id=device, device_id_type=pl.DeviceIdType.MESH,
        )

    def skipped(u):
        return hb if u // 2 in DIAGONAL and u % 2 == 1 else 0

    def cut(ref, u):
        slot, low = u // 2, u % 2
        (r0, c0), (r1, c1) = OWNED[0][slot], OWNED[1][slot]
        row = r0 if r0 == r1 else r0 + (r1 - r0) * c
        col = c0 if c0 == c1 else c0 + (c1 - c0) * c
        skip = skipped(u)
        start = pl.multiple_of(((col + 2 * c) % 4) * bs + skip, hb)
        return ref.at[pl.ds(pl.multiple_of(row * bs + low * hb, hb), hb), pl.ds(start, bs - skip)]

    def unit(ref, owner, u):
        skip = skipped(u)
        return ref.at[owner, u // 2, pl.ds(u % 2 * hb, hb), pl.ds(skip, bs - skip)]

    def relay_unit(u):
        skip = skipped(u)
        return relay_cov.at[u // 2, pl.ds(u % 2 * hb, hb), pl.ds(skip, bs - skip)]

    def far_copy(i):
        rows = pl.ds(i * cr, cr)
        return remote(gain_in.at[rows], far.at[c, rows], s_far.at[i], r_far.at[i], side)

    def far_cross(i, slot):
        rows = pl.ds(i * cr, cr)
        return remote(far.at[slot, rows], far.at[slot, rows], s_farx.at[i], r_farx.at[i], core)

    def near_copy(u):
        return remote(cut(cov_in, u), unit(near_cov, c, u), s_near.at[u], r_near.at[u], side)

    def near_g_copy():
        return remote(sent_g, near_g, s_near.at[UNITS], r_near.at[UNITS], side)

    def near_cross(u, owner):
        part = unit(near_cov, owner, u)
        return remote(part, part, s_nearx.at[u], r_nearx.at[u], core)

    def prod_cross(n, slot):
        cols = pl.ds(n * bs, bs)
        return remote(weight.at[slot, :, cols], weight.at[slot, :, cols], s_prod.at[n], r_prod.at[n], core)

    def chain_copy(u):
        return remote(cut(cov_out, u), unit(chain_cov, c, u), s_chain.at[u], r_chain.at[u], below)

    def relay_copy(u):
        return remote(cut(cov_out, u), relay_unit(u), s_chain.at[u], r_relay.at[u], side)

    def relay_down(u):
        return remote(relay_unit(u), unit(chain_cov, c, u), s_relay.at[u], r_chain.at[u], below)

    def chain_g_copy():
        return remote(sent_g, chain_g, s_chain.at[UNITS], r_chain.at[UNITS], below)

    def chain_side(u):
        part = unit(chain_cov, c, u)
        return remote(part, part, s_side.at[u], r_chain.at[u], side)

    def chain_g_side():
        return remote(chain_g, chain_g, s_side.at[UNITS], r_chain.at[UNITS], side)

    def chain_cross(u, owner):
        part = unit(chain_cov, owner, u)
        return remote(part, part, s_chainx.at[u], r_chainx.at[u], core)

    def start_in_turn(copy, sequence, k, window=WINDOW):
        if k >= window:
            copy(sequence[k - window]).wait_send()
        copy(sequence[k]).start()

    def combine(left, later, later_g, emit, emit_g):
        for owner in range(2):
            for slot in DIAGONAL:
                later[owner, slot, hb:, :hb] = later[owner, slot, :hb, hb:].T
        for j in range(4):
            total = None
            for i in range(4):
                piece = left[c, :, i * bs : (i + 1) * bs]
                if (i, j) in TABLE:
                    term = dot(piece, later[TABLE[(i, j)]])
                else:
                    term = dot_t(piece, later[TABLE[(j, i)]])
                total = term if total is None else total + term
            cross[:half, j * bs : (j + 1) * bs] = total.astype(jnp.bfloat16)
        row = to_row(later_g[...]).astype(jnp.bfloat16)
        cross[half:, :] = jnp.broadcast_to(row, (16, width))
        for n in range(4):
            panel = (n // 2 + c) % 2
            cols = pl.ds(pl.multiple_of(((n + 2 * c) % 4) * bs, bs), bs)
            rows = left[panel, (n % 2) * bs : (n % 2 + 1) * bs, :]
            out = dot_t(cross[...], rows)
            emit(n, cols, out[:half])
            emit_g(cols, out[half : half + 1])

    def first(left, later, later_g):
        def emit(n, cols, value):
            added[:, cols] = value + cov[:, cols].astype(jnp.float32)

        def emit_g(cols, value):
            added_g[:, cols] = value + offset[:, cols].astype(jnp.float32)

        combine(left, later, later_g, emit, emit_g)

    def finish(left, later, later_g):
        go_down = jnp.logical_and(even, z > 0)
        around = jnp.logical_and(go_down, z < last_z)
        straight = jnp.logical_and(go_down, top)

        def emit(n, cols, value):
            cov_out[:, cols] = (value + added[:, cols]).astype(jnp.bfloat16)
            ready = [2 * slot + low for slot in ((0,), (1, 2), (3,), (4,))[n] for low in range(2)]

            @pl.when(around)
            def _():
                for u in ready:
                    if u in ROUND:
                        relay_copy(u).start()
                    else:
                        start_in_turn(chain_copy, DIRECT, DIRECT.index(u))

            @pl.when(straight)
            def _():
                for u in ready:
                    start_in_turn(chain_copy, range(UNITS), u)

        def emit_g(cols, value):
            added_g[:, cols] = value + added_g[:, cols]

        combine(left, later, later_g, emit, emit_g)
        mean_out[...] = added_g[...].astype(jnp.bfloat16)

        @pl.when(go_down)
        def _():
            sent_g[...] = to_tile(added_g[...])
            chain_g_copy().start()
            chain_g_copy().wait_send()

        @pl.when(around)
        def _():
            for u in ROUND + DIRECT[-WINDOW:]:
                chain_copy(u).wait_send()

        @pl.when(straight)
        def _():
            for u in range(UNITS)[-WINDOW:]:
                chain_copy(u).wait_send()

    def plain_added():
        added[...] = cov[...].astype(jnp.float32)
        added_g[...] = offset[...].astype(jnp.float32)

    def receive(order, forwarded):
        for u in order:
            chain_copy(u).wait_recv()
            chain_cross(u, c).start()
            if u in forwarded:
                chain_side(u).start()

    def receive_near(units):
        for u in units:
            near_copy(u).wait_recv()
            near_cross(u, c).start()

    @pl.when(odd)
    def _():
        sent_g[...] = to_tile(offset[...].astype(jnp.float32))
        near_g_copy().start()

        @pl.when(z < last_z)
        def _():
            for i in range(2):
                far_copy(i).start()
            swap = remote(gain_in, weight.at[c], s_own.at[0], r_own.at[0], core)
            swap.start()
            load_cov.wait()
            pltpu.make_async_copy(gain_in, weight.at[c], s_local.at[1]).wait()
            plain_added()
            for i in range(2, CHUNKS):
                start_in_turn(far_copy, range(CHUNKS), i, 2)
            for i in range(CHUNKS)[-2:]:
                far_copy(i).wait_send()
                start_in_turn(near_copy, range(UNITS), i - CHUNKS + 2)
            swap.wait()

        @pl.when(top)
        def _():
            for u in range(2):
                near_copy(u).start()
            load_cov.wait()
            pltpu.make_async_copy(gain_in, weight.at[c], s_local.at[1]).wait()
            cov_out[...] = cov[...]
            mean_out[...] = offset[...]

        for u in range(2, UNITS):
            start_in_turn(near_copy, range(UNITS), u)

        @pl.when(z < last_z)
        def _():
            @pl.when(second)
            def _():
                receive(range(UNITS), ())

            @pl.when(jnp.logical_not(second))
            def _():
                receive(ODD_ORDER, ROUND)

            chain_g_copy().wait_recv()

            @pl.when(z > 0)
            def _():
                for u in ROUND:
                    relay_copy(u).wait_recv()
                    relay_down(u).start()

    @pl.when(even)
    def _():
        swap = remote(gain_in, own.at[c], s_own.at[0], r_own.at[0], core)
        swap.start()
        load_cov.wait()
        pltpu.make_async_copy(gain_in, own.at[c], s_local.at[1]).wait()

        @pl.when(z < last_z)
        def _():
            for i in range(CHUNKS):
                far_copy(i).wait_recv()
                far_cross(i, c).start()
            for i in range(CHUNKS):
                far_cross(i, 1 - c).wait_recv()
            for n in range(4):
                cols = slice(n * bs, (n + 1) * bs)
                value = dot(own[c, :, :half], far[0, :, cols]) + dot(own[c, :, half:], far[1, :, cols])
                weight[c, :, cols] = value.astype(jnp.bfloat16)
                prod_cross(n, c).start()

        swap.wait()

        @pl.when(second)
        def _():
            receive(range(UNITS), range(UNITS))
            chain_g_copy().wait_recv()
            chain_g_side().start()
            receive_near(range(5))
            for n in range(4):
                prod_cross(n, 1 - c).wait_recv()
            for u in range(UNITS):
                chain_cross(u, 1 - c).wait_recv()
            first(weight, chain_cov, chain_g)
            receive_near(range(5, UNITS))

        @pl.when(jnp.logical_not(second))
        def _():
            receive_near(range(UNITS))

        near_g_copy().wait_recv()
        for u in range(UNITS):
            near_cross(u, 1 - c).wait_recv()

        @pl.when(z < last_z - 1)
        def _():
            first(own, near_cov, near_g)
            receive(EVEN_ORDER, DIRECT)
            chain_g_copy().wait_recv()
            chain_g_side().start()
            for n in range(4):
                prod_cross(n, 1 - c).wait_recv()

        @pl.when(top)
        def _():
            plain_added()

        @pl.when(z >= last_z - 1)
        def _():
            finish(own, near_cov, near_g)

    @pl.when(jnp.logical_or(z < last_z - 1, jnp.logical_and(odd, second)))
    def _():
        for u in range(UNITS):
            chain_cross(u, 1 - c).wait_recv()
        finish(weight, chain_cov, chain_g)

    @pl.when(z < last_z)
    def _():
        for u in range(UNITS):
            chain_cross(u, c).wait_send()

    @pl.when(even)
    def _():
        for u in range(UNITS):
            near_cross(u, c).wait_send()

        @pl.when(z < last_z)
        def _():
            chain_g_side().wait_send()
            for u in DIRECT:
                chain_side(u).wait_send()
            for n in range(4):
                prod_cross(n, c).wait_send()
            for i in range(CHUNKS):
                far_cross(i, c).wait_send()

        @pl.when(second)
        def _():
            for u in ROUND:
                chain_side(u).wait_send()

    @pl.when(odd)
    def _():
        for u in range(UNITS)[-WINDOW:]:
            near_copy(u).wait_send()
        near_g_copy().wait_send()

        @pl.when(jnp.logical_and(z < last_z, z > 0))
        def _():
            for u in ROUND:
                relay_down(u).wait_send()

        @pl.when(z < last_z - 1)
        def _():
            for u in ROUND:
                chain_side(u).wait_send()


def body(gain, offset, residual_cov):
    steps = lax.axis_size("tm")
    _, half, width = gain.shape
    bs = width // 4
    bf16, f32 = jnp.bfloat16, jnp.float32
    hbm = pl.BlockSpec(memory_space=pltpu.HBM)
    vmem = pl.BlockSpec(memory_space=pltpu.VMEM)
    counts = (2, 1, 1) + (CHUNKS,) * 4 + (UNITS + 1,) * 4 + (4, 4) + (UNITS + 1,) * 7
    mean, cov = pl.pallas_call(
        functools.partial(kernel, steps),
        out_shape=(
            jax.ShapeDtypeStruct((1, width), bf16),
            jax.ShapeDtypeStruct((half, width), bf16),
        ),
        in_specs=[hbm, vmem, hbm],
        out_specs=(vmem, vmem),
        scratch_shapes=[
            pltpu.VMEM((2, half, width), bf16),
            pltpu.VMEM((2, half, width), bf16),
            pltpu.VMEM((2, half, width), bf16),
            pltpu.VMEM((2, 5, bs, bs), bf16),
            pltpu.VMEM((2, 5, bs, bs), bf16),
            pltpu.VMEM((2, bs, bs), bf16),
            pltpu.VMEM((half, width), bf16),
            pltpu.VMEM((8, width // 8), f32),
            pltpu.VMEM((8, width // 8), f32),
            pltpu.VMEM((8, width // 8), f32),
            pltpu.VMEM((half + 16, width), bf16),
            pltpu.VMEM((half, width), f32),
            pltpu.VMEM((1, width), f32),
        ]
        + [pltpu.SemaphoreType.DMA((n,)) for n in counts],
        compiler_params=pltpu.CompilerParams(
            collective_id=0, has_side_effects=True, vmem_limit_bytes=40 * 2**20
        ),
        cost_estimate=pl.CostEstimate(
            flops=10 * half * width * width, bytes_accessed=6 * half * width, transcendentals=0
        ),
    )(gain[0], offset, residual_cov[0])
    return mean, cov[None]


def solution(mesh):
    in_specs = (
        P(("parts", "tm"), "panel", None),
        P(("parts", "tm"), None),
        P(("parts", "tm"), "panel", None),
    )
    out_specs = (P(("parts", "tm"), None), P(("parts", "tm"), "panel", None))
    return jax.shard_map(body, mesh=mesh, in_specs=in_specs, out_specs=out_specs, check_vma=False)
```

```python
import functools

import jax
import jax.numpy as jnp
from jax import lax
from jax.experimental import pallas as pl
from jax.experimental.pallas import tpu as pltpu
from jax.sharding import PartitionSpec as P

OWNED = (((0, 0), (0, 1), (1, 1), (1, 2), (0, 2)), ((0, 0), (0, 1), (1, 1), (1, 2), (1, 3)))
CHUNKS = 4
UNITS = 10
DIAGONAL = (0, 2)
ROUND = (0, 1)
DIRECT = (2, 3, 4, 5, 6, 7, 8, 9)
EVEN_ORDER = (2, 3, 4, 5, 6, 7, 0, 1, 8, 9)
ODD_ORDER = (0, 1, 2, 3, 4, 5, 6, 7, 8, 9)
WINDOW = 3


def block_table():
    table = {}
    for core in range(2):
        for slot, (row, col) in enumerate(OWNED[core]):
            table[(2 * core + row, (2 * core + col) % 4)] = (core, slot)
    return table


TABLE = block_table()


def dot(a, b):
    return jnp.dot(a, b, preferred_element_type=jnp.float32)


def dot_t(a, b):
    return lax.dot_general(a, b, (((1,), (1,)), ((), ())), preferred_element_type=jnp.float32)


def to_tile(row):
    lanes = row.shape[1] // 8
    return jnp.concatenate([row[:, i * lanes : (i + 1) * lanes] for i in range(8)], axis=0)


def to_row(tile):
    return jnp.concatenate([tile[i : i + 1, :] for i in range(8)], axis=1)


def kernel(
    steps, gain_in, offset, cov_in, mean_out, cov_out,
    own, far, weight, near_cov, chain_cov, relay_cov, cov,
    near_g, chain_g, sent_g, cross, added, added_g,
    s_local, s_own, r_own, s_far, r_far, s_farx, r_farx, s_near, r_near, s_nearx, r_nearx,
    s_prod, r_prod, s_chain, r_chain, s_chainx, r_chainx, s_side, s_relay, r_relay,
):
    t = lax.axis_index("tm")
    c = lax.axis_index("panel")
    z = t // 2
    y = t % 2
    last_z = steps // 2 - 1
    half, width = cov.shape
    bs = width // 4
    hb = bs // 2
    cr = half // CHUNKS

    core = {"panel": 1 - c}
    side = {"tm": t + 1 - 2 * y}
    above = {"tm": t + 2}
    below = {"tm": t - 2}
    even = y == 0
    odd = y == 1
    top = z == last_z
    second = z == last_z - 1

    load_cov = pltpu.make_async_copy(cov_in, cov, s_local.at[0])
    load_cov.start()

    @pl.when(even)
    def _():
        pltpu.make_async_copy(gain_in, own.at[c], s_local.at[1]).start()

    @pl.when(odd)
    def _():
        pltpu.make_async_copy(gain_in, weight.at[c], s_local.at[1]).start()

    barrier = pltpu.get_barrier_semaphore()
    pl.semaphore_signal(barrier, inc=1, device_id=core)
    pl.semaphore_signal(barrier, inc=1, device_id=side)

    @pl.when(z < last_z)
    def _():
        pl.semaphore_signal(barrier, inc=1, device_id=above)

    @pl.when(z > 0)
    def _():
        pl.semaphore_signal(barrier, inc=1, device_id=below)

    pl.semaphore_wait(barrier, 2 + jnp.where(z < last_z, 1, 0) + jnp.where(z > 0, 1, 0))

    def remote(src, dst, send, recv, device):
        return pltpu.make_async_remote_copy(
            src_ref=src, dst_ref=dst, send_sem=send, recv_sem=recv,
            device_id=device, device_id_type=pl.DeviceIdType.MESH,
        )

    def skipped(u):
        return hb if u // 2 in DIAGONAL and u % 2 == 1 else 0

    def cut(ref, u):
        slot, low = u // 2, u % 2
        (r0, c0), (r1, c1) = OWNED[0][slot], OWNED[1][slot]
        row = r0 if r0 == r1 else r0 + (r1 - r0) * c
        col = c0 if c0 == c1 else c0 + (c1 - c0) * c
        skip = skipped(u)
        start = pl.multiple_of(((col + 2 * c) % 4) * bs + skip, hb)
        return ref.at[pl.ds(pl.multiple_of(row * bs + low * hb, hb), hb), pl.ds(start, bs - skip)]

    def unit(ref, owner, u):
        skip = skipped(u)
        return ref.at[owner, u // 2, pl.ds(u % 2 * hb, hb), pl.ds(skip, bs - skip)]

    def relay_unit(u):
        skip = skipped(u)
        return relay_cov.at[u // 2, pl.ds(u % 2 * hb, hb), pl.ds(skip, bs - skip)]

    def far_copy(i):
        rows = pl.ds(i * cr, cr)
        return remote(gain_in.at[rows], far.at[c, rows], s_far.at[i], r_far.at[i], side)

    def far_cross(i, slot):
        rows = pl.ds(i * cr, cr)
        return remote(far.at[slot, rows], far.at[slot, rows], s_farx.at[i], r_farx.at[i], core)

    def near_copy(u):
        return remote(cut(cov_in, u), unit(near_cov, c, u), s_near.at[u], r_near.at[u], side)

    def near_g_copy():
        return remote(sent_g, near_g, s_near.at[UNITS], r_near.at[UNITS], side)

    def near_cross(u, owner):
        part = unit(near_cov, owner, u)
        return remote(part, part, s_nearx.at[u], r_nearx.at[u], core)

    def prod_cross(n, slot):
        cols = pl.ds(n * bs, bs)
        return remote(weight.at[slot, :, cols], weight.at[slot, :, cols], s_prod.at[n], r_prod.at[n], core)

    def chain_copy(u):
        return remote(cut(cov_out, u), unit(chain_cov, c, u), s_chain.at[u], r_chain.at[u], below)

    def relay_copy(u):
        return remote(cut(cov_out, u), relay_unit(u), s_chain.at[u], r_relay.at[u], side)

    def relay_down(u):
        return remote(relay_unit(u), unit(chain_cov, c, u), s_relay.at[u], r_chain.at[u], below)

    def chain_g_copy():
        return remote(sent_g, chain_g, s_chain.at[UNITS], r_chain.at[UNITS], below)

    def chain_side(u):
        part = unit(chain_cov, c, u)
        return remote(part, part, s_side.at[u], r_chain.at[u], side)

    def chain_g_side():
        return remote(chain_g, chain_g, s_side.at[UNITS], r_chain.at[UNITS], side)

    def chain_cross(u, owner):
        part = unit(chain_cov, owner, u)
        return remote(part, part, s_chainx.at[u], r_chainx.at[u], core)

    def start_in_turn(copy, sequence, k, window=WINDOW):
        if k >= window:
            copy(sequence[k - window]).wait_send()
        copy(sequence[k]).start()

    def combine(left, later, later_g, emit, emit_g, between=None):
        for owner in range(2):
            for slot in DIAGONAL:
                later[owner, slot, hb:, :hb] = later[owner, slot, :hb, hb:].T
        for j in range(4):
            total = None
            for i in range(4):
                piece = left[c, :, i * bs : (i + 1) * bs]
                if (i, j) in TABLE:
                    term = dot(piece, later[TABLE[(i, j)]])
                else:
                    term = dot_t(piece, later[TABLE[(j, i)]])
                total = term if total is None else total + term
            cross[:half, j * bs : (j + 1) * bs] = total.astype(jnp.bfloat16)
        if between is not None:
            between()
        row = to_row(later_g[...]).astype(jnp.bfloat16)
        cross[half:, :] = jnp.broadcast_to(row, (16, width))
        for n in range(4):
            panel = (n // 2 + c) % 2
            cols = pl.ds(pl.multiple_of(((n + 2 * c) % 4) * bs, bs), bs)
            rows = left[panel, (n % 2) * bs : (n % 2 + 1) * bs, :]
            out = dot_t(cross[...], rows)
            emit(n, cols, out[:half])
            emit_g(cols, out[half : half + 1])

    def first(left, later, later_g, between=None):
        def emit(n, cols, value):
            added[:, cols] = value + cov[:, cols].astype(jnp.float32)

        def emit_g(cols, value):
            added_g[:, cols] = value + offset[:, cols].astype(jnp.float32)

        combine(left, later, later_g, emit, emit_g, between)

    def finish(left, later, later_g):
        go_down = jnp.logical_and(even, z > 0)
        around = jnp.logical_and(go_down, z < last_z)
        straight = jnp.logical_and(go_down, top)

        def emit(n, cols, value):
            cov_out[:, cols] = (value + added[:, cols]).astype(jnp.bfloat16)
            ready = [2 * slot + low for slot in ((0,), (1, 2), (3,), (4,))[n] for low in range(2)]

            @pl.when(around)
            def _():
                for u in ready:
                    if u in ROUND:
                        relay_copy(u).start()
                    else:
                        start_in_turn(chain_copy, DIRECT, DIRECT.index(u))

            @pl.when(straight)
            def _():
                for u in ready:
                    start_in_turn(chain_copy, range(UNITS), u)

        def emit_g(cols, value):
            added_g[:, cols] = value + added_g[:, cols]

        combine(left, later, later_g, emit, emit_g)
        mean_out[...] = added_g[...].astype(jnp.bfloat16)

        @pl.when(go_down)
        def _():
            sent_g[...] = to_tile(added_g[...])
            chain_g_copy().start()
            chain_g_copy().wait_send()

        @pl.when(around)
        def _():
            for u in ROUND + DIRECT[-WINDOW:]:
                chain_copy(u).wait_send()

        @pl.when(straight)
        def _():
            for u in range(UNITS)[-WINDOW:]:
                chain_copy(u).wait_send()

    def plain_added():
        added[...] = cov[...].astype(jnp.float32)
        added_g[...] = offset[...].astype(jnp.float32)

    def receive(order, forwarded):
        for u in order:
            chain_copy(u).wait_recv()
            chain_cross(u, c).start()
            if u in forwarded:
                chain_side(u).start()

    def receive_near(units):
        for u in units:
            near_copy(u).wait_recv()
            near_cross(u, c).start()

    @pl.when(odd)
    def _():
        sent_g[...] = to_tile(offset[...].astype(jnp.float32))
        near_g_copy().start()

        @pl.when(z < last_z)
        def _():
            for i in range(2):
                far_copy(i).start()
            swap = remote(gain_in, weight.at[c], s_own.at[0], r_own.at[0], core)
            swap.start()
            load_cov.wait()
            pltpu.make_async_copy(gain_in, weight.at[c], s_local.at[1]).wait()
            plain_added()
            for i in range(2, CHUNKS):
                start_in_turn(far_copy, range(CHUNKS), i, 2)
            for i in range(CHUNKS)[-2:]:
                far_copy(i).wait_send()
                start_in_turn(near_copy, range(UNITS), i - CHUNKS + 2)
            swap.wait()

        @pl.when(top)
        def _():
            for u in range(2):
                near_copy(u).start()
            load_cov.wait()
            pltpu.make_async_copy(gain_in, weight.at[c], s_local.at[1]).wait()
            cov_out[...] = cov[...]
            mean_out[...] = offset[...]

        for u in range(2, UNITS):
            start_in_turn(near_copy, range(UNITS), u)

        @pl.when(z < last_z)
        def _():
            @pl.when(second)
            def _():
                receive(range(UNITS), ())

            @pl.when(jnp.logical_not(second))
            def _():
                receive(ODD_ORDER, ROUND)

            chain_g_copy().wait_recv()

            @pl.when(z > 0)
            def _():
                for u in ROUND:
                    relay_copy(u).wait_recv()
                    relay_down(u).start()

    @pl.when(even)
    def _():
        swap = remote(gain_in, own.at[c], s_own.at[0], r_own.at[0], core)
        swap.start()
        load_cov.wait()
        pltpu.make_async_copy(gain_in, own.at[c], s_local.at[1]).wait()

        @pl.when(z < last_z)
        def _():
            for i in range(CHUNKS):
                far_copy(i).wait_recv()
                far_cross(i, c).start()
            for i in range(CHUNKS):
                far_cross(i, 1 - c).wait_recv()
            for n in range(4):
                cols = slice(n * bs, (n + 1) * bs)
                value = dot(own[c, :, :half], far[0, :, cols]) + dot(own[c, :, half:], far[1, :, cols])
                weight[c, :, cols] = value.astype(jnp.bfloat16)
                prod_cross(n, c).start()

        swap.wait()

        @pl.when(second)
        def _():
            receive(range(UNITS), range(UNITS))
            chain_g_copy().wait_recv()
            chain_g_side().start()
            receive_near(range(5))
            for n in range(4):
                prod_cross(n, 1 - c).wait_recv()
            for u in range(UNITS):
                chain_cross(u, 1 - c).wait_recv()
            first(weight, chain_cov, chain_g, lambda: receive_near(range(5, UNITS)))

        @pl.when(jnp.logical_not(second))
        def _():
            receive_near(range(UNITS))

        near_g_copy().wait_recv()
        for u in range(UNITS):
            near_cross(u, 1 - c).wait_recv()

        @pl.when(z < last_z - 1)
        def _():
            first(own, near_cov, near_g)
            receive(EVEN_ORDER, DIRECT)
            chain_g_copy().wait_recv()
            chain_g_side().start()
            for n in range(4):
                prod_cross(n, 1 - c).wait_recv()

        @pl.when(top)
        def _():
            plain_added()

        @pl.when(z >= last_z - 1)
        def _():
            finish(own, near_cov, near_g)

    @pl.when(jnp.logical_or(z < last_z - 1, jnp.logical_and(odd, second)))
    def _():
        for u in range(UNITS):
            chain_cross(u, 1 - c).wait_recv()
        finish(weight, chain_cov, chain_g)

    @pl.when(z < last_z)
    def _():
        for u in range(UNITS):
            chain_cross(u, c).wait_send()

    @pl.when(even)
    def _():
        for u in range(UNITS):
            near_cross(u, c).wait_send()

        @pl.when(z < last_z)
        def _():
            chain_g_side().wait_send()
            for u in DIRECT:
                chain_side(u).wait_send()
            for n in range(4):
                prod_cross(n, c).wait_send()
            for i in range(CHUNKS):
                far_cross(i, c).wait_send()

        @pl.when(second)
        def _():
            for u in ROUND:
                chain_side(u).wait_send()

    @pl.when(odd)
    def _():
        for u in range(UNITS)[-WINDOW:]:
            near_copy(u).wait_send()
        near_g_copy().wait_send()

        @pl.when(jnp.logical_and(z < last_z, z > 0))
        def _():
            for u in ROUND:
                relay_down(u).wait_send()

        @pl.when(z < last_z - 1)
        def _():
            for u in ROUND:
                chain_side(u).wait_send()


def body(gain, offset, residual_cov):
    steps = lax.axis_size("tm")
    _, half, width = gain.shape
    bs = width // 4
    bf16, f32 = jnp.bfloat16, jnp.float32
    hbm = pl.BlockSpec(memory_space=pltpu.HBM)
    vmem = pl.BlockSpec(memory_space=pltpu.VMEM)
    counts = (2, 1, 1) + (CHUNKS,) * 4 + (UNITS + 1,) * 4 + (4, 4) + (UNITS + 1,) * 7
    mean, cov = pl.pallas_call(
        functools.partial(kernel, steps),
        out_shape=(
            jax.ShapeDtypeStruct((1, width), bf16),
            jax.ShapeDtypeStruct((half, width), bf16),
        ),
        in_specs=[hbm, vmem, hbm],
        out_specs=(vmem, vmem),
        scratch_shapes=[
            pltpu.VMEM((2, half, width), bf16),
            pltpu.VMEM((2, half, width), bf16),
            pltpu.VMEM((2, half, width), bf16),
            pltpu.VMEM((2, 5, bs, bs), bf16),
            pltpu.VMEM((2, 5, bs, bs), bf16),
            pltpu.VMEM((2, bs, bs), bf16),
            pltpu.VMEM((half, width), bf16),
            pltpu.VMEM((8, width // 8), f32),
            pltpu.VMEM((8, width // 8), f32),
            pltpu.VMEM((8, width // 8), f32),
            pltpu.VMEM((half + 16, width), bf16),
            pltpu.VMEM((half, width), f32),
            pltpu.VMEM((1, width), f32),
        ]
        + [pltpu.SemaphoreType.DMA((n,)) for n in counts],
        compiler_params=pltpu.CompilerParams(
            collective_id=0, has_side_effects=True, vmem_limit_bytes=63 * 2**20
        ),
        cost_estimate=pl.CostEstimate(
            flops=10 * half * width * width, bytes_accessed=6 * half * width, transcendentals=0
        ),
    )(gain[0], offset, residual_cov[0])
    return mean, cov[None]


def solution(mesh):
    in_specs = (
        P(("parts", "tm"), "panel", None),
        P(("parts", "tm"), None),
        P(("parts", "tm"), "panel", None),
    )
    out_specs = (P(("parts", "tm"), None), P(("parts", "tm"), "panel", None))
    return jax.shard_map(body, mesh=mesh, in_specs=in_specs, out_specs=out_specs, check_vma=False)
```

```python
import functools

import jax
import jax.numpy as jnp
from jax import lax
from jax.experimental import pallas as pl
from jax.experimental.pallas import tpu as pltpu
from jax.sharding import PartitionSpec as P

OWNED = (((0, 0), (0, 1), (1, 1), (1, 2), (0, 2)), ((0, 0), (0, 1), (1, 1), (1, 2), (1, 3)))
CHUNKS = 4
UNITS = 10
DIAGONAL = (0, 2)
ROUND = (0, 1)
DIRECT = (2, 3, 4, 5, 6, 7, 8, 9)
EVEN_ORDER = (2, 3, 4, 5, 0, 6, 1, 7, 8, 9)
ODD_ORDER = (0, 1, 2, 3, 4, 5, 6, 7, 8, 9)
WINDOW = 3


def block_table():
    table = {}
    for core in range(2):
        for slot, (row, col) in enumerate(OWNED[core]):
            table[(2 * core + row, (2 * core + col) % 4)] = (core, slot)
    return table


TABLE = block_table()


def dot(a, b):
    return jnp.dot(a, b, preferred_element_type=jnp.float32)


def dot_t(a, b):
    return lax.dot_general(a, b, (((1,), (1,)), ((), ())), preferred_element_type=jnp.float32)


def to_tile(row):
    lanes = row.shape[1] // 8
    return jnp.concatenate([row[:, i * lanes : (i + 1) * lanes] for i in range(8)], axis=0)


def to_row(tile):
    return jnp.concatenate([tile[i : i + 1, :] for i in range(8)], axis=1)


def kernel(
    steps, gain_in, offset, cov_in, mean_out, cov_out,
    own, far, weight, near_cov, chain_cov, relay_cov, cov,
    near_g, chain_g, sent_g, cross, added, added_g,
    s_local, s_own, r_own, s_far, r_far, s_farx, r_farx, s_near, r_near, s_nearx, r_nearx,
    s_prod, r_prod, s_chain, r_chain, s_chainx, r_chainx, s_side, s_relay, r_relay,
):
    t = lax.axis_index("tm")
    c = lax.axis_index("panel")
    z = t // 2
    y = t % 2
    last_z = steps // 2 - 1
    half, width = cov.shape
    bs = width // 4
    hb = bs // 2
    cr = half // CHUNKS

    core = {"panel": 1 - c}
    side = {"tm": t + 1 - 2 * y}
    above = {"tm": t + 2}
    below = {"tm": t - 2}
    even = y == 0
    odd = y == 1
    top = z == last_z
    second = z == last_z - 1

    load_cov = pltpu.make_async_copy(cov_in, cov, s_local.at[0])
    load_cov.start()

    @pl.when(even)
    def _():
        pltpu.make_async_copy(gain_in, own.at[c], s_local.at[1]).start()

    @pl.when(odd)
    def _():
        pltpu.make_async_copy(gain_in, weight.at[c], s_local.at[1]).start()

    barrier = pltpu.get_barrier_semaphore()
    pl.semaphore_signal(barrier, inc=1, device_id=core)
    pl.semaphore_signal(barrier, inc=1, device_id=side)

    @pl.when(z < last_z)
    def _():
        pl.semaphore_signal(barrier, inc=1, device_id=above)

    @pl.when(z > 0)
    def _():
        pl.semaphore_signal(barrier, inc=1, device_id=below)

    pl.semaphore_wait(barrier, 2 + jnp.where(z < last_z, 1, 0) + jnp.where(z > 0, 1, 0))

    def remote(src, dst, send, recv, device):
        return pltpu.make_async_remote_copy(
            src_ref=src, dst_ref=dst, send_sem=send, recv_sem=recv,
            device_id=device, device_id_type=pl.DeviceIdType.MESH,
        )

    def skipped(u):
        return hb if u // 2 in DIAGONAL and u % 2 == 1 else 0

    def cut(ref, u):
        slot, low = u // 2, u % 2
        (r0, c0), (r1, c1) = OWNED[0][slot], OWNED[1][slot]
        row = r0 if r0 == r1 else r0 + (r1 - r0) * c
        col = c0 if c0 == c1 else c0 + (c1 - c0) * c
        skip = skipped(u)
        start = pl.multiple_of(((col + 2 * c) % 4) * bs + skip, hb)
        return ref.at[pl.ds(pl.multiple_of(row * bs + low * hb, hb), hb), pl.ds(start, bs - skip)]

    def unit(ref, owner, u):
        skip = skipped(u)
        return ref.at[owner, u // 2, pl.ds(u % 2 * hb, hb), pl.ds(skip, bs - skip)]

    def relay_unit(u):
        skip = skipped(u)
        return relay_cov.at[u // 2, pl.ds(u % 2 * hb, hb), pl.ds(skip, bs - skip)]

    def far_copy(i):
        rows = pl.ds(i * cr, cr)
        return remote(gain_in.at[rows], far.at[c, rows], s_far.at[i], r_far.at[i], side)

    def far_cross(i, slot):
        rows = pl.ds(i * cr, cr)
        return remote(far.at[slot, rows], far.at[slot, rows], s_farx.at[i], r_farx.at[i], core)

    def near_copy(u):
        return remote(cut(cov_in, u), unit(near_cov, c, u), s_near.at[u], r_near.at[u], side)

    def near_g_copy():
        return remote(sent_g, near_g, s_near.at[UNITS], r_near.at[UNITS], side)

    def near_cross(u, owner):
        part = unit(near_cov, owner, u)
        return remote(part, part, s_nearx.at[u], r_nearx.at[u], core)

    def prod_cross(n, slot):
        cols = pl.ds(n * bs, bs)
        return remote(weight.at[slot, :, cols], weight.at[slot, :, cols], s_prod.at[n], r_prod.at[n], core)

    def chain_copy(u):
        return remote(cut(cov_out, u), unit(chain_cov, c, u), s_chain.at[u], r_chain.at[u], below)

    def relay_copy(u):
        return remote(cut(cov_out, u), relay_unit(u), s_chain.at[u], r_relay.at[u], side)

    def relay_down(u):
        return remote(relay_unit(u), unit(chain_cov, c, u), s_relay.at[u], r_chain.at[u], below)

    def chain_g_copy():
        return remote(sent_g, chain_g, s_chain.at[UNITS], r_chain.at[UNITS], below)

    def chain_side(u):
        part = unit(chain_cov, c, u)
        return remote(part, part, s_side.at[u], r_chain.at[u], side)

    def chain_g_side():
        return remote(chain_g, chain_g, s_side.at[UNITS], r_chain.at[UNITS], side)

    def chain_cross(u, owner):
        part = unit(chain_cov, owner, u)
        return remote(part, part, s_chainx.at[u], r_chainx.at[u], core)

    def start_in_turn(copy, sequence, k, window=WINDOW):
        if k >= window:
            copy(sequence[k - window]).wait_send()
        copy(sequence[k]).start()

    def combine(left, later, later_g, emit, emit_g):
        for owner in range(2):
            for slot in DIAGONAL:
                later[owner, slot, hb:, :hb] = later[owner, slot, :hb, hb:].T
        for j in range(4):
            total = None
            for i in range(4):
                piece = left[c, :, i * bs : (i + 1) * bs]
                if (i, j) in TABLE:
                    term = dot(piece, later[TABLE[(i, j)]])
                else:
                    term = dot_t(piece, later[TABLE[(j, i)]])
                total = term if total is None else total + term
            cross[:half, j * bs : (j + 1) * bs] = total.astype(jnp.bfloat16)
        row = to_row(later_g[...]).astype(jnp.bfloat16)
        cross[half:, :] = jnp.broadcast_to(row, (16, width))
        for n in range(4):
            panel = (n // 2 + c) % 2
            cols = pl.ds(pl.multiple_of(((n + 2 * c) % 4) * bs, bs), bs)
            rows = left[panel, (n % 2) * bs : (n % 2 + 1) * bs, :]
            out = dot_t(cross[...], rows)
            emit(n, cols, out[:half])
            emit_g(cols, out[half : half + 1])

    def first(left, later, later_g):
        def emit(n, cols, value):
            added[:, cols] = value + cov[:, cols].astype(jnp.float32)

        def emit_g(cols, value):
            added_g[:, cols] = value + offset[:, cols].astype(jnp.float32)

        combine(left, later, later_g, emit, emit_g)

    def finish(left, later, later_g):
        go_down = jnp.logical_and(even, z > 0)
        around = jnp.logical_and(go_down, z < last_z)
        straight = jnp.logical_and(go_down, top)

        def emit(n, cols, value):
            cov_out[:, cols] = (value + added[:, cols]).astype(jnp.bfloat16)
            ready = [2 * slot + low for slot in ((0,), (1, 2), (3,), (4,))[n] for low in range(2)]

            @pl.when(around)
            def _():
                for u in ready:
                    if u in ROUND:
                        relay_copy(u).start()
                    else:
                        start_in_turn(chain_copy, DIRECT, DIRECT.index(u))

            @pl.when(straight)
            def _():
                for u in ready:
                    start_in_turn(chain_copy, range(UNITS), u)

        def emit_g(cols, value):
            added_g[:, cols] = value + added_g[:, cols]

        combine(left, later, later_g, emit, emit_g)
        mean_out[...] = added_g[...].astype(jnp.bfloat16)

        @pl.when(go_down)
        def _():
            sent_g[...] = to_tile(added_g[...])
            chain_g_copy().start()
            chain_g_copy().wait_send()

        @pl.when(around)
        def _():
            for u in ROUND + DIRECT[-WINDOW:]:
                chain_copy(u).wait_send()

        @pl.when(straight)
        def _():
            for u in range(UNITS)[-WINDOW:]:
                chain_copy(u).wait_send()

    def plain_added():
        added[...] = cov[...].astype(jnp.float32)
        added_g[...] = offset[...].astype(jnp.float32)

    def receive(order, forwarded):
        for u in order:
            chain_copy(u).wait_recv()
            chain_cross(u, c).start()
            if u in forwarded:
                chain_side(u).start()

    def receive_near(units):
        for u in units:
            near_copy(u).wait_recv()
            near_cross(u, c).start()

    @pl.when(odd)
    def _():
        sent_g[...] = to_tile(offset[...].astype(jnp.float32))
        near_g_copy().start()

        @pl.when(z < last_z)
        def _():
            for i in range(2):
                far_copy(i).start()
            swap = remote(gain_in, weight.at[c], s_own.at[0], r_own.at[0], core)
            swap.start()
            load_cov.wait()
            pltpu.make_async_copy(gain_in, weight.at[c], s_local.at[1]).wait()
            plain_added()
            for i in range(2, CHUNKS):
                start_in_turn(far_copy, range(CHUNKS), i, 2)
            for i in range(CHUNKS)[-2:]:
                far_copy(i).wait_send()
                start_in_turn(near_copy, range(UNITS), i - CHUNKS + 2)
            swap.wait()

        @pl.when(top)
        def _():
            for u in range(2):
                near_copy(u).start()
            load_cov.wait()
            pltpu.make_async_copy(gain_in, weight.at[c], s_local.at[1]).wait()
            cov_out[...] = cov[...]
            mean_out[...] = offset[...]

        for u in range(2, UNITS):
            start_in_turn(near_copy, range(UNITS), u)

        @pl.when(z < last_z)
        def _():
            @pl.when(second)
            def _():
                receive(range(UNITS), ())

            @pl.when(jnp.logical_not(second))
            def _():
                receive(ODD_ORDER, ROUND)

            chain_g_copy().wait_recv()

            @pl.when(z > 0)
            def _():
                for u in ROUND:
                    relay_copy(u).wait_recv()
                    relay_down(u).start()

    @pl.when(even)
    def _():
        swap = remote(gain_in, own.at[c], s_own.at[0], r_own.at[0], core)
        swap.start()
        load_cov.wait()
        pltpu.make_async_copy(gain_in, own.at[c], s_local.at[1]).wait()

        @pl.when(z < last_z)
        def _():
            for i in range(CHUNKS):
                far_copy(i).wait_recv()
                far_cross(i, c).start()
            for i in range(CHUNKS):
                far_cross(i, 1 - c).wait_recv()
            for n in range(4):
                cols = slice(n * bs, (n + 1) * bs)
                value = dot(own[c, :, :half], far[0, :, cols]) + dot(own[c, :, half:], far[1, :, cols])
                weight[c, :, cols] = value.astype(jnp.bfloat16)
                prod_cross(n, c).start()

        swap.wait()

        @pl.when(second)
        def _():
            receive(range(UNITS), range(UNITS))
            chain_g_copy().wait_recv()
            chain_g_side().start()
            receive_near(range(5))
            for n in range(4):
                prod_cross(n, 1 - c).wait_recv()
            for u in range(UNITS):
                chain_cross(u, 1 - c).wait_recv()
            first(weight, chain_cov, chain_g)
            receive_near(range(5, UNITS))

        @pl.when(jnp.logical_not(second))
        def _():
            receive_near(range(UNITS))

        near_g_copy().wait_recv()
        for u in range(UNITS):
            near_cross(u, 1 - c).wait_recv()

        @pl.when(z < last_z - 1)
        def _():
            first(own, near_cov, near_g)
            receive(EVEN_ORDER, DIRECT)
            chain_g_copy().wait_recv()
            chain_g_side().start()
            for n in range(4):
                prod_cross(n, 1 - c).wait_recv()

        @pl.when(top)
        def _():
            plain_added()

        @pl.when(z >= last_z - 1)
        def _():
            finish(own, near_cov, near_g)

    @pl.when(jnp.logical_or(z < last_z - 1, jnp.logical_and(odd, second)))
    def _():
        for u in range(UNITS):
            chain_cross(u, 1 - c).wait_recv()
        finish(weight, chain_cov, chain_g)

    @pl.when(z < last_z)
    def _():
        for u in range(UNITS):
            chain_cross(u, c).wait_send()

    @pl.when(even)
    def _():
        for u in range(UNITS):
            near_cross(u, c).wait_send()

        @pl.when(z < last_z)
        def _():
            chain_g_side().wait_send()
            for u in DIRECT:
                chain_side(u).wait_send()
            for n in range(4):
                prod_cross(n, c).wait_send()
            for i in range(CHUNKS):
                far_cross(i, c).wait_send()

        @pl.when(second)
        def _():
            for u in ROUND:
                chain_side(u).wait_send()

    @pl.when(odd)
    def _():
        for u in range(UNITS)[-WINDOW:]:
            near_copy(u).wait_send()
        near_g_copy().wait_send()

        @pl.when(jnp.logical_and(z < last_z, z > 0))
        def _():
            for u in ROUND:
                relay_down(u).wait_send()

        @pl.when(z < last_z - 1)
        def _():
            for u in ROUND:
                chain_side(u).wait_send()


def body(gain, offset, residual_cov):
    steps = lax.axis_size("tm")
    _, half, width = gain.shape
    bs = width // 4
    bf16, f32 = jnp.bfloat16, jnp.float32
    hbm = pl.BlockSpec(memory_space=pltpu.HBM)
    vmem = pl.BlockSpec(memory_space=pltpu.VMEM)
    counts = (2, 1, 1) + (CHUNKS,) * 4 + (UNITS + 1,) * 4 + (4, 4) + (UNITS + 1,) * 7
    mean, cov = pl.pallas_call(
        functools.partial(kernel, steps),
        out_shape=(
            jax.ShapeDtypeStruct((1, width), bf16),
            jax.ShapeDtypeStruct((half, width), bf16),
        ),
        in_specs=[hbm, vmem, hbm],
        out_specs=(vmem, vmem),
        scratch_shapes=[
            pltpu.VMEM((2, half, width), bf16),
            pltpu.VMEM((2, half, width), bf16),
            pltpu.VMEM((2, half, width), bf16),
            pltpu.VMEM((2, 5, bs, bs), bf16),
            pltpu.VMEM((2, 5, bs, bs), bf16),
            pltpu.VMEM((2, bs, bs), bf16),
            pltpu.VMEM((half, width), bf16),
            pltpu.VMEM((8, width // 8), f32),
            pltpu.VMEM((8, width // 8), f32),
            pltpu.VMEM((8, width // 8), f32),
            pltpu.VMEM((half + 16, width), bf16),
            pltpu.VMEM((half, width), f32),
            pltpu.VMEM((1, width), f32),
        ]
        + [pltpu.SemaphoreType.DMA((n,)) for n in counts],
        compiler_params=pltpu.CompilerParams(
            collective_id=0, has_side_effects=True, vmem_limit_bytes=40 * 2**20
        ),
        cost_estimate=pl.CostEstimate(
            flops=10 * half * width * width, bytes_accessed=6 * half * width, transcendentals=0
        ),
    )(gain[0], offset, residual_cov[0])
    return mean, cov[None]


def solution(mesh):
    in_specs = (
        P(("parts", "tm"), "panel", None),
        P(("parts", "tm"), None),
        P(("parts", "tm"), "panel", None),
    )
    out_specs = (P(("parts", "tm"), None), P(("parts", "tm"), "panel", None))
    return jax.shard_map(body, mesh=mesh, in_specs=in_specs, out_specs=out_specs, check_vma=False)
```
